32 devices in a mesh: groups: 2 (over y), tensor: 4 (over z), store: 4 (over x, core).
Axes of the slice: x: 2, y: 2, z: 4, core: 2. Of those that a mesh axis runs over, the one named last changes fastest.
Arguments:
- gate: bfloat16 [768, 28672], P(('groups', 'store'), 'tensor'), parts along dimension 0, may hold values from -6 to 6
- up: bfloat16 [768, 28672], P(('groups', 'store'), 'tensor'), parts along dimension 0, may hold values from -6 to 6
- down_weight: bfloat16 [28672, 8192], P('tensor', 'store'), may hold values from -0.03125 to 0.03125
- shrink_weights: bfloat16 [32, 28672, 64], P('store', 'tensor'), may hold values from -0.03125 to 0.03125
- expand_weights: bfloat16 [32, 64, 8192], P(None, 'tensor', 'store'), may hold values from -0.75 to 0.75
- row_adapter_index: int32 [768, 1], P('groups'), parts along dimension 0, may hold values from 0 to 31; in each aligned block of 96 rows (0 to 95, 96 to 191, ...) at most 4 rows name the same one
- residual: bfloat16 [768, 8192], P(('groups', 'tensor'), 'store'), parts along dimension 0, may hold values from -6 to 6
Outputs:
- mixed: bfloat16 [768, 8192], P(('groups', 'tensor'), 'store'), parts along dimension 0
The draws below stay inside these ranges and needn't reach their ends.
There are 2 independent parts, one for each index of `groups`. The reference program is written for one: setup_inputs(seed, part) draws one part's arguments, and reference() takes and returns one part's arrays. A program takes and returns all parts, laid end to end along the dimension named above; an argument that names none is the same for every part. Nothing has to cross between parts.
Inputs may be any that keep to these rules, and one draw needn't show every extreme that they name: `row_adapter_index`: in each aligned block of 96 rows no adapter is named by more than 4 rows.
All inputs are finite; a program needn't handle non-finite values.
Results may differ from the reference program's by a relative error of at most 0.0043.
Values may be sent and summed in bfloat16 or wider, within the bound.
A program may use at most 192 MiB of HBM per device.

```python
import math
import jax
import jax.numpy as jnp
import numpy as np
from jax import lax

MODEL_WIDTH = 8192
HIDDEN_UNITS = 28672
ADAPTER_RANK = 64
MOST = 4
ROWS_DEV = 96
ROWS = 384
ADAPTER_COUNT = 32


def steps_of(own_key, shape, cuts, least, high):
    def one(dim, shards_of):
        draws = jax.random.uniform(jax.random.fold_in(jax.random.fold_in(own_key, 6), dim), (shards_of,), jnp.float32, least / len(cuts), high / len(cuts))
        return jnp.repeat(jnp.exp(draws), shape[dim] // shards_of).reshape((-1,) + (1,) * (len(shape) - dim - 1))

    factor_of = one(*cuts[0])
    for cut in cuts[1:]:
        factor_of = factor_of * one(*cut)
    return factor_of


def routed_block(key, own, number, rows, count, top, bound, slope):
    sequence = jax.random.permutation(key, count)
    crowded, usual = portions_of(count, rows * top, bound, slope, True), portions_of(count, rows * top, bound, slope, False)
    places = jnp.arange(count)

    def named(tallies, rotation):
        used = int((tallies > 0).sum())
        fixed = max(1, used // 4)
        moved = fixed + (places - fixed + rotation * (used - fixed)) % max(1, count - fixed)
        return jnp.zeros((count,), jnp.int32).at[sequence[jnp.where(places < fixed, places, moved)]].set(jnp.asarray(tallies, jnp.int32))

    tallies = jnp.where(number % 4 == 0, named(crowded, number // 4), named(usual, number - number // 4 - 1))
    mixed = jax.random.permutation(jax.random.fold_in(own, 3), count)
    donor, taker = mixed[0:count // 2 * 2:2], mixed[1:count // 2 * 2:2]
    room = jnp.minimum(tallies[donor] - 1, bound - tallies[taker]) // 2
    room = jnp.where((donor == sequence[0]) | (taker == sequence[0]) | (tallies[taker] == 0), 0, jnp.maximum(room, 0))
    moved = jax.random.randint(jax.random.fold_in(own, 4), (count // 2,), 0, 1 << 20) % (room + 1)
    tallies = tallies.at[donor].add(-moved).at[taker].add(moved)
    labels = jnp.searchsorted(jnp.cumsum(tallies), jnp.arange(rows * top), side="right").astype(jnp.int32)
    grid = labels.reshape(top, rows).T
    grid = grid[jax.random.permutation(jax.random.fold_in(own, 1), rows)]
    rotation = jax.random.randint(jax.random.fold_in(own, 2), (rows, 1), 0, top)
    return jnp.take_along_axis(grid, (jnp.arange(top)[None, :] + rotation) % top, axis=1)


def portions_of(count, total, most, slope, full):
    portions = [(1 << 20) // math.isqrt(rank ** slope) + 1 for rank in range(1, count + 1)]
    largest = most if full else min(most, max(-(-total // count), total * portions[0] // sum(portions)))
    least = 1 if total - largest >= count - 1 else 0
    counts, rest = [largest] + [least] * (count - 1), total - largest - least * (count - 1)
    while rest > 0:
        movable = [i for i in range(1, count) if counts[i] < largest] or [i for i in range(1, count) if counts[i] < most]
        pool, left = sum([portions[i] for i in movable]), rest
        for i in movable:
            extra = min(most - counts[i], max(1, left * portions[i] // pool), rest)
            counts[i] = counts[i] + extra
            rest = rest - extra
    return np.array(counts)


def normal_values(rng, dims, width, reach, split=(), kind=jnp.bfloat16):
    loudness = steps_of(rng, dims, split, -0.22, 0.18) if split else 1.0
    array = jax.random.normal(rng, dims, jnp.float32) * width * loudness
    return jnp.minimum(jnp.maximum(array, -reach), reach).astype(kind)


def setup_inputs(seed: int = 0, part: int = 0) -> dict:
    arg_keys = jax.random.split(jax.random.key(seed), 8)
    part_splits = jax.random.split(jax.random.fold_in(arg_keys[7], part), 8)
    gate = normal_values(part_splits[0], (ROWS, HIDDEN_UNITS), 1.0, 6.0, ((0, 4), (1, 4)))
    up = normal_values(part_splits[1], (ROWS, HIDDEN_UNITS), 1.0, 6.0, ((0, 4), (1, 4)))
    down_weight = normal_values(arg_keys[2], (HIDDEN_UNITS, MODEL_WIDTH), HIDDEN_UNITS ** -0.5, 0.03125, ((0, 4), (1, 4)))
    shrink_weights = normal_values(arg_keys[3], (ADAPTER_COUNT, HIDDEN_UNITS, ADAPTER_RANK), HIDDEN_UNITS ** -0.5, 0.03125, ((0, 4), (1, 4)))
    expand_weights = normal_values(arg_keys[4], (ADAPTER_COUNT, ADAPTER_RANK, MODEL_WIDTH), ADAPTER_RANK ** -0.5, 0.75, ((1, 4), (2, 4)))
    row_adapter_index_keys = jax.random.split(jax.random.fold_in(part_splits[5], 1), ROWS // ROWS_DEV)
    row_adapter_index_turns = jax.random.permutation(jax.random.fold_in(part_splits[5], 3), ROWS // ROWS_DEV)
    row_adapter_index = jax.vmap(lambda own, number: routed_block(jax.random.fold_in(part_splits[5], 2), own, number, ROWS_DEV, ADAPTER_COUNT, 1, MOST, 2))(row_adapter_index_keys, row_adapter_index_turns).reshape((ROWS, 1))
    residual = normal_values(part_splits[6], (ROWS, MODEL_WIDTH), 1.0, 6.0, ((0, 4), (1, 4)))
    return {"gate": gate, "up": up, "down_weight": down_weight, "shrink_weights": shrink_weights, "expand_weights": expand_weights, "row_adapter_index": row_adapter_index, "residual": residual}


def reference(gate, up, down_weight, shrink_weights, expand_weights, row_adapter_index, residual):
    hidden = (jax.nn.silu(gate.astype(jnp.float32)) * up.astype(jnp.float32)).astype(jnp.bfloat16)
    row_ids = row_adapter_index[:, 0].astype(jnp.int32)

    def one_row(pair):
        row, adapter_index = pair
        shrink_matrix = lax.dynamic_index_in_dim(shrink_weights, adapter_index, 0, keepdims=False).astype(jnp.float32)
        shrunk = jnp.dot(row.astype(jnp.float32), shrink_matrix, precision=lax.Precision.HIGHEST)
        shrunk = shrunk.astype(jnp.bfloat16).astype(jnp.float32)
        expand_matrix = lax.dynamic_index_in_dim(expand_weights, adapter_index, 0, keepdims=False).astype(jnp.float32)
        return jnp.dot(shrunk, expand_matrix, precision=lax.Precision.HIGHEST)

    delta = lax.map(one_row, (hidden, row_ids))
    base = jnp.dot(hidden.astype(jnp.float32), down_weight.astype(jnp.float32), precision=lax.Precision.HIGHEST)
    return (residual.astype(jnp.float32) + (base + delta)).astype(jnp.bfloat16)
```

```python
import jax
import jax.numpy as jnp
from jax import lax
from jax.sharding import PartitionSpec as P


def shards(gate, up, down_weight, shrink_weights, expand_weights, row_adapter_index, residual):
    hidden = (jax.nn.silu(gate.astype(jnp.float32)) * up.astype(jnp.float32)).astype(jnp.bfloat16)
    adapters_here = shrink_weights.shape[0]
    adapter_table = expand_weights.shape[0]
    device_rank = expand_weights.shape[1]
    all_ids = row_adapter_index[:, 0]
    hidden_all = lax.all_gather(hidden, "store", axis=0, tiled=True)
    local = lax.axis_index("store") * adapters_here + jnp.arange(adapters_here, dtype=jnp.int32)
    part = jnp.einsum("rf,afk->ark", hidden_all, shrink_weights, preferred_element_type=jnp.float32)
    named = local[:, None] == all_ids[None, :]
    partial_value = jnp.sum(jnp.where(named[:, :, None], part, 0.0), axis=0)
    summed = lax.psum(partial_value, ("tensor", "store"))
    shrink_all = lax.dynamic_slice_in_dim(
        summed, lax.axis_index("tensor") * device_rank, device_rank, 1
    ).astype(jnp.bfloat16)
    flattened_expand = expand_weights.reshape(adapter_table * device_rank, expand_weights.shape[2])
    select = (all_ids[:, None] == jnp.arange(adapter_table, dtype=jnp.int32)[None, :]).astype(
        jnp.bfloat16
    )
    expand_in = (select[:, :, None] * shrink_all[:, None, :]).reshape(
        all_ids.shape[0], adapter_table * device_rank
    )
    base = jnp.dot(hidden_all, down_weight, preferred_element_type=jnp.float32)
    delta = jnp.dot(expand_in, flattened_expand, preferred_element_type=jnp.float32)
    total = lax.psum_scatter(
        (base + delta).astype(jnp.bfloat16), "tensor", scatter_dimension=0, tiled=True
    )
    return (residual.astype(jnp.float32) + total.astype(jnp.float32)).astype(jnp.bfloat16)


def solution(mesh):
    in_specs = (
        P(("groups", "store"), "tensor"),
        P(("groups", "store"), "tensor"),
        P("tensor", "store"),
        P("store", "tensor", None),
        P(None, "tensor", "store"),
        P("groups", None),
        P(("groups", "tensor"), "store"),
    )
    out_specs = P(("groups", "tensor"), "store")
    return jax.shard_map(shards, mesh=mesh, in_specs=in_specs, out_specs=out_specs, check_vma=False)
```

```python
import functools
import jax
import jax.numpy as jnp
from jax import lax
from jax.experimental import pallas as pl
from jax.experimental.pallas import tpu as pltpu
from jax.sharding import PartitionSpec as P

PIECES = 2
TILE = 512
F32, BF16 = jnp.float32, jnp.bfloat16


def kernel(T, pieces, *refs):
    gate, up, down_hbm, shrink_hbm, expand_hbm, residual, ids_cols, ids_rows, out = refs[:9]
    down, shrink, expand, hid, base, snd, from_left, from_right = refs[9:17]
    parts, z_got, q_own, q_got = refs[17:21]
    load_sem, h_send, h_recv, z_send, z_recv, q_send, q_recv, c_send, c_recv_l, c_recv_r = refs[21:]
    rows, ffd = gate.shape
    wide = down.shape[1]
    piece = rows // pieces
    rank = parts.shape[1]
    adapters_here = shrink_hbm.shape[0] // rank
    device_rank = rank // T
    units = 2 * pieces

    t = lax.axis_index("tensor")
    s = lax.axis_index("store")
    chip, core = s // 2, s % 2
    sib = 2 * chip + 1 - core
    peer = 2 * (1 - chip) + core
    dia = 2 * (1 - chip) + 1 - core
    left, right = (t + T - 1) % T, (t + 1) % T

    loads = [
        pltpu.make_async_copy(a, b, load_sem.at[i])
        for i, (a, b) in enumerate(((shrink_hbm, shrink), (down_hbm, down), (expand_hbm, expand)))
    ]
    for load in loads:
        load.start()

    barrier = pltpu.get_barrier_semaphore()
    for k in range(1, T):
        pl.semaphore_signal(
            barrier, inc=1, device_id={"tensor": (t + k) % T}, device_id_type=pl.DeviceIdType.MESH
        )
    for k in range(1, 4):
        pl.semaphore_signal(
            barrier, inc=1, device_id={"store": (s + k) % 4}, device_id_type=pl.DeviceIdType.MESH
        )
    pl.semaphore_wait(barrier, T - 1 + 3)

    def remote(src, dst, send, recv, device):
        return pltpu.make_async_remote_copy(
            src_ref=src,
            dst_ref=dst,
            send_sem=send,
            recv_sem=recv,
            device_id=device,
            device_id_type=pl.DeviceIdType.MESH,
        )

    def hidden_copy(kind, block, j, device):
        ref = hid.at[block, pl.ds(j * piece, piece)]
        return remote(ref, ref, h_send.at[kind, j], h_recv.at[kind, j], {"store": device})

    step = 1024 if ffd % 1024 == 0 else ffd
    for j in range(pieces):
        here = slice(j * piece, (j + 1) * piece)

        def columns(i, _, here=here):
            at = pl.ds(pl.multiple_of(i * step, 128), step)
            g = gate[here, at].astype(F32)
            hid[s, here, at] = (g / (1.0 + jnp.exp(-g)) * up[here, at].astype(F32)).astype(BF16)
            return 0

        lax.fori_loop(0, ffd // step, columns, 0)
        hidden_copy(0, s, j, peer).start()
        hidden_copy(1, s, j, sib).start()

    def unit_rows(u):
        chip_of, j = (chip if u < pieces else 1 - chip), u % pieces
        return 2 * chip_of, slice(j * piece, (j + 1) * piece), piece

    def lhs(where):
        first, here, n = where
        return hid[pl.ds(first, 2), here, :].reshape(2 * n, ffd)

    def shrink_part(u):
        ids = ids_rows[u]
        half = adapters_here // 2
        total = None
        for h in range(2):
            part = lax.dot_general(
                shrink[h * half * rank : (h + 1) * half * rank, :],
                lhs(unit_rows(u)),
                (((1,), (1,)), ((), ())),
                preferred_element_type=F32,
            )
            for a in range(half):
                mine = jnp.where(
                    ids == s * adapters_here + h * half + a, part[a * rank : (a + 1) * rank], 0.0
                )
                total = mine if total is None else total + mine
        parts[u] = total
        for k in range(1, T):
            z_copy(u, k).start()

    def z_copy(u, k):
        to = (t + k) % T
        return remote(
            parts.at[u, pl.ds(pl.multiple_of(to * device_rank, 8), device_rank)],
            z_got.at[u, k - 1],
            z_send.at[u, k - 1],
            z_recv.at[u, k - 1],
            {"tensor": to},
        )

    def q_copy(u, k):
        to = u if k == 0 else (u + pieces) % units
        return remote(
            q_own.at[u], q_got.at[to, k], q_send.at[u, k], q_recv.at[to, k],
            {"store": (sib, peer, dia)[k]},
        )

    def q_wait(u, k):
        remote(
            q_own.at[u], q_got.at[u, k], q_send.at[u, k], q_recv.at[u, k],
            {"store": (sib, peer, dia)[k]},
        ).wait_recv()

    def shrink_sum(u):
        total = parts[u, pl.ds(pl.multiple_of(t * device_rank, 8), device_rank), :]
        for k in range(1, T):
            z_copy(u, k).wait_recv()
            total = total + z_got[u, k - 1]
        q_own[u] = total
        for k in range(3):
            q_copy(u, k).start()

    def product(where, lo, hi):
        first, here, n = where

        def tile(i, _):
            at = pl.ds(pl.multiple_of(i * TILE, 128), TILE)
            value = jnp.dot(lhs(where), down[:, at], preferred_element_type=F32)
            base[pl.ds(first, 2), here, at] = value.reshape(2, n, TILE)
            return 0

        lax.fori_loop(lo, hi, tile, 0)

    def delta(u):
        first, here, n = unit_rows(u)
        total = q_own[u]
        for k in range(3):
            q_wait(u, k)
            total = total + q_got[u, k]
        low = total.T.astype(BF16)
        slots = expand.shape[0]
        spread = (
            lax.broadcasted_iota(jnp.int32, (device_rank, slots), 1) % device_rank
            == lax.broadcasted_iota(jnp.int32, (device_rank, slots), 0)
        )
        wide_low = jnp.dot(low, jnp.where(spread, 1.0, 0.0).astype(BF16), preferred_element_type=F32)
        named = (
            lax.broadcasted_iota(jnp.int32, (2 * n, slots), 1) // device_rank == ids_cols[u]
        )
        expand_in = jnp.where(named, wide_low, 0.0).astype(BF16)

        def tile(i, _):
            at = pl.ds(pl.multiple_of(i * TILE, 128), TILE)
            value = jnp.dot(expand_in, expand[:, at], preferred_element_type=F32)
            base[pl.ds(first, 2), here, at] += value.reshape(2, n, TILE)
            return 0

        lax.fori_loop(0, wide // TILE, tile, 0)

    def chain(u, i, to_right):
        first, here, n = unit_rows(u)
        place = (first + i, pl.ds(here.start, n))
        into = from_left if to_right else from_right
        got = c_recv_l if to_right else c_recv_r
        return remote(
            snd.at[place], into.at[place], c_send.at[u, i], got.at[u, i],
            {"tensor": right if to_right else left},
        )

    def hop(u, middle):
        first, here, n = unit_rows(u)
        for i in range(2):
            b = first + i
            for to_right in (True, False):
                onward = (t < b) if to_right else (t > b)
                end = (t == 0) if to_right else (t == T - 1)
                inner = (t > 0) if to_right else (t < T - 1)

                @pl.when(onward & (inner if middle else end))
                def _(i=i, b=b, to_right=to_right):
                    value = base[b, here, :]
                    if middle:
                        chain(u, i, to_right).wait_recv()
                        got = from_left if to_right else from_right
                        value = value + got[b, here, :].astype(F32)
                    snd[b, here, :] = value.astype(BF16)
                    chain(u, i, to_right).start()

    def finish(u):
        first, here, n = unit_rows(u)
        for i in range(2):
            b = first + i

            @pl.when(t == b)
            def _(i=i, b=b):
                base[b, here, :] += residual[here, :].astype(F32)

                @pl.when(t > 0)
                def _():
                    chain(u, i, True).wait_recv()
                    base[b, here, :] += from_left[b, here, :].astype(F32)

                @pl.when(t < T - 1)
                def _():
                    chain(u, i, False).wait_recv()
                    base[b, here, :] += from_right[b, here, :].astype(F32)

                out[here, :] = base[b, here, :].astype(BF16)

            @pl.when(t != b)
            def _(i=i):
                chain(u, i, True).wait_send()

    tiles = wide // TILE
    near = (2 * chip, slice(0, rows), rows)
    for j in range(pieces):
        hidden_copy(1, sib, j, sib).wait_recv()
    loads[0].wait()
    for j in range(pieces):
        shrink_part(j)
    loads[1].wait()
    product(near, 0, tiles // 2)
    for j in range(pieces):
        shrink_sum(j)
    product(near, tiles // 2, tiles)
    loads[2].wait()
    for j in range(pieces):
        u = pieces + j
        hidden_copy(0, peer, j, peer).wait_recv()
        hidden_copy(2, peer, j, sib).start()
        hidden_copy(2, dia, j, sib).wait_recv()
        shrink_part(u)
        product(unit_rows(u), 0, tiles // 2)
        shrink_sum(u)
        if j > 0:
            hop(j - 1, True)
            hop(u - 1, True)
        product(unit_rows(u), tiles // 2, tiles)
        delta(j)
        hop(j, False)
        delta(u)
        hop(u, False)
    hop(pieces - 1, True)
    hop(units - 1, True)
    for u in range(units):
        finish(u)
    for j in range(pieces):
        hidden_copy(0, s, j, peer).wait_send()
        hidden_copy(1, s, j, sib).wait_send()
        hidden_copy(2, peer, j, sib).wait_send()
    for u in range(units):
        for k in range(1, T):
            z_copy(u, k).wait_send()
        for k in range(3):
            q_copy(u, k).wait_send()


def fused(T, gate, up, down_weight, shrink_weights, expand_weights, row_adapter_index, residual):
    rows, ffd = gate.shape
    wide = down_weight.shape[1]
    adapters_here, _, rank = shrink_weights.shape
    table, device_rank, _ = expand_weights.shape
    pieces = PIECES
    piece = rows // pieces
    shrink = jnp.swapaxes(shrink_weights, 1, 2).reshape(adapters_here * rank, ffd)
    expand = expand_weights.reshape(table * device_rank, wide)
    chip = lax.axis_index("store") // 2
    ids = row_adapter_index.reshape(2, 2, pieces, piece)
    ids = jnp.where(chip == 0, ids, ids[::-1]).transpose(0, 2, 1, 3).reshape(2 * pieces, 2 * piece)
    units = 2 * pieces
    vmem = pl.BlockSpec(memory_space=pltpu.VMEM)
    hbm = pl.BlockSpec(memory_space=pl.ANY)
    dma = pltpu.SemaphoreType.DMA
    return pl.pallas_call(
        functools.partial(kernel, T, pieces),
        out_shape=jax.ShapeDtypeStruct((rows, wide), BF16),
        in_specs=[vmem, vmem, hbm, hbm, hbm, vmem] + [vmem, vmem],
        out_specs=vmem,
        scratch_shapes=[
            pltpu.VMEM((ffd, wide), BF16),
            pltpu.VMEM((adapters_here * rank, ffd), BF16),
            pltpu.VMEM((table * device_rank, wide), BF16),
            pltpu.VMEM((4, rows, ffd), BF16),
            pltpu.VMEM((4, rows, wide), F32),
            pltpu.VMEM((4, rows, wide), BF16),
            pltpu.VMEM((4, rows, wide), BF16),
            pltpu.VMEM((4, rows, wide), BF16),
        ]
        + [
            pltpu.VMEM((units, rank, 2 * piece), F32),
            pltpu.VMEM((units, T - 1, device_rank, 2 * piece), F32),
            pltpu.VMEM((units, device_rank, 2 * piece), F32),
            pltpu.VMEM((units, 3, device_rank, 2 * piece), F32),
            dma((3,)),
            dma((3, pieces)),
            dma((3, pieces)),
            dma((units, T - 1)),
            dma((units, T - 1)),
            dma((units, 3)),
            dma((units, 3)),
            dma((units, 2)),
            dma((units, 2)),
            dma((units, 2)),
        ],
        compiler_params=pltpu.CompilerParams(
            collective_id=0, has_side_effects=True, vmem_limit_bytes=62 * 2**20
        ),
    )(
        gate, up, down_weight, shrink, expand, residual,
        ids[:, :, None], ids[:, None, :],
    )


def shards(gate, up, down_weight, shrink_weights, expand_weights, row_adapter_index, residual):
    hidden = (jax.nn.silu(gate.astype(jnp.float32)) * up.astype(jnp.float32)).astype(jnp.bfloat16)
    adapters_here = shrink_weights.shape[0]
    adapter_table = expand_weights.shape[0]
    device_rank = expand_weights.shape[1]
    all_ids = row_adapter_index[:, 0]
    hidden_all = lax.all_gather(hidden, "store", axis=0, tiled=True)
    local = lax.axis_index("store") * adapters_here + jnp.arange(adapters_here, dtype=jnp.int32)
    part = jnp.einsum("rf,afk->ark", hidden_all, shrink_weights, preferred_element_type=jnp.float32)
    named = local[:, None] == all_ids[None, :]
    partial_value = jnp.sum(jnp.where(named[:, :, None], part, 0.0), axis=0)
    summed = lax.psum(partial_value, ("tensor", "store"))
    shrink_all = lax.dynamic_slice_in_dim(
        summed, lax.axis_index("tensor") * device_rank, device_rank, 1
    ).astype(jnp.bfloat16)
    flattened_expand = expand_weights.reshape(adapter_table * device_rank, expand_weights.shape[2])
    select = (all_ids[:, None] == jnp.arange(adapter_table, dtype=jnp.int32)[None, :]).astype(
        jnp.bfloat16
    )
    expand_in = (select[:, :, None] * shrink_all[:, None, :]).reshape(
        all_ids.shape[0], adapter_table * device_rank
    )
    base = jnp.dot(hidden_all, down_weight, preferred_element_type=jnp.float32)
    delta = jnp.dot(expand_in, flattened_expand, preferred_element_type=jnp.float32)
    total = lax.psum_scatter(
        (base + delta).astype(jnp.bfloat16), "tensor", scatter_dimension=0, tiled=True
    )
    return (residual.astype(jnp.float32) + total.astype(jnp.float32)).astype(jnp.bfloat16)


def solution(mesh):
    tensor, store = mesh.shape["tensor"], mesh.shape["store"]
    in_specs = (
        P(("groups", "store"), "tensor"),
        P(("groups", "store"), "tensor"),
        P("tensor", "store"),
        P("store", "tensor", None),
        P(None, "tensor", "store"),
        P("groups", None),
        P(("groups", "tensor"), "store"),
    )
    out_specs = P(("groups", "tensor"), "store")
    body = functools.partial(fused, tensor) if tensor == 4 and store == 4 else shards
    return jax.shard_map(body, mesh=mesh, in_specs=in_specs, out_specs=out_specs, check_vma=False)
```
